32 devices in a mesh: patch: 8 (over y, x, core), mlp: 4 (over z).
Axes of the slice: x: 2, y: 2, z: 4, core: 2. Of those that a mesh axis runs over, the one named last changes fastest.
Arguments:
- latent: bfloat16 [2048, 2432], P('patch', 'mlp'), may hold values from -24 to 24
- split_list: int32 [8, 4], P('patch'), may hold values from 0 to 256, as said below
- modulation: float32 [1, 6, 2432], replicated, may hold values from -3 to 3
- w_qkv: bfloat16 [2432, 3, 1536], P(None, None, 'mlp'), may hold values from -0.125 to 0.125
- w_out: bfloat16 [1536, 2432], P('mlp'), may hold values from -0.15625 to 0.15625
- w_up: bfloat16 [2432, 5120], P(None, 'mlp'), may hold values from -0.125 to 0.125
- w_down: bfloat16 [5120, 2432], P('mlp'), may hold values from -0.078125 to 0.078125
- qk_gains: float32 [3, 64], replicated, may hold values from 1.6 to 2.4
- text_kv: bfloat16 [2, 1, 154, 1536], P(None, None, None, 'mlp'), may hold values from -6 to 6
- timestep: int32 [1], replicated, may hold values from 0 to 27
- step_sizes: float32 [28], replicated, may hold values from -0.6 to -0.1
Outputs:
- latent_next: bfloat16 [2048, 2432], P('patch', 'mlp')
The draws below stay inside these ranges and needn't reach their ends.
Inputs may be any that keep to these rules, and one draw needn't show every extreme that they name: `split_list`: row d holds device d's tile pieces (item, count, item, count); over all devices the counts of every item add up to 1024. A device's two counts add up to at most 256, to exactly 256 on some device and to 0 on another. The devices holding an item's tokens form a run of consecutive indices of patch, taken cyclically. Both pieces may name the same item; they are then two parts of it.
All inputs are finite; a program needn't handle non-finite values.
Results may differ from the reference program's by a relative error of at most 0.0049.
Values may be sent and summed in bfloat16 or wider, within the bound.
A program may use at most 128 MiB of HBM per device.

```python
import jax
import jax.numpy as jnp
from jax import lax

D = 2432
HEADS = 24
HEAD = 64
FF = 5120
IMG = 1024
TXT = 154
CAP = 256
STEPS = 28
ITEMS = 1
SLOTS = 2048
N_PATCH = 8


def draw_latent(key, part):
    keys_all = jax.random.split(key, 3)
    row_scale = 10.0 ** jax.random.uniform(keys_all[0], (SLOTS, 1), minval=-0.25, maxval=0.25)
    col_scale = 10.0 ** jax.random.uniform(keys_all[1], (1, D), minval=-0.5, maxval=0.5)
    base = jnp.clip(jax.random.normal(keys_all[2], (SLOTS, D)), -4.0, 4.0)
    return (base * row_scale * col_scale).astype(jnp.float32).astype(jnp.bfloat16)


def draw_split_list(key, part):
    keys_all = jax.random.split(key, 4)
    pairs = N_PATCH // 2
    first_loads = jax.random.randint(keys_all[0], (pairs,), CAP // 8, CAP - CAP // 8 + 1)
    forced = jax.random.randint(keys_all[1], (), 0, pairs)
    first_loads = jnp.where(jnp.arange(pairs, dtype=jnp.int32) == forced, CAP, first_loads).astype(jnp.int32)
    loads = jnp.stack([first_loads, CAP - first_loads], axis=1).reshape(N_PATCH).astype(jnp.int32)
    before = jnp.cumsum(loads, dtype=jnp.int32) - loads
    offset = jax.random.randint(keys_all[2], (), 0, IMG).astype(jnp.int32)
    order = jax.random.permutation(keys_all[3], ITEMS).astype(jnp.int32)
    total_rows = ITEMS * IMG
    start_pos = (before + offset) % total_rows
    first_item = start_pos // IMG
    count_a = jnp.minimum(loads, IMG - start_pos % IMG)
    count_b = loads - count_a
    item_a = order[first_item]
    item_b = order[(first_item + 1) % ITEMS]
    return jnp.stack([item_a, count_a, item_b, count_b], axis=1).astype(jnp.int32)


def block_levels(rng, extent, pieces, low, top_value):
    gain = 1.0
    for position, blocks in pieces:
        steps = jax.random.uniform(jax.random.fold_in(jax.random.fold_in(rng, 6), position), (blocks,), jnp.float32, low / len(pieces), top_value / len(pieces))
        gain = gain * jnp.repeat(jnp.exp(steps), extent[position] // blocks).reshape((-1,) + (1,) * (len(extent) - 1 - position))
    return gain


def scatter_about(own_key, shape, width, reach, shards=(), held_as=jnp.bfloat16):
    result = jax.random.normal(own_key, shape, jnp.float32) * width
    if len(shards) > 0:
        result = block_levels(own_key, shape, shards, -0.22, 0.18) * result
    return jnp.clip(result, min=-reach, max=reach).astype(held_as)


def setup_inputs(seed: int = 0) -> dict:
    streams_of = jax.random.split(jax.random.key(seed), 12)
    latent = draw_latent(jax.random.fold_in(streams_of[11], 71), 0)
    split_list = draw_split_list(jax.random.fold_in(streams_of[11], 71), 0)
    modulation = scatter_about(streams_of[2], (ITEMS, 6, D), 0.6, 3.0, (), jnp.float32)
    w_qkv = scatter_about(streams_of[3], (D, 3, HEADS * HEAD), D ** -0.5, 0.125, ((2, 4),))
    w_out = scatter_about(streams_of[4], (HEADS * HEAD, D), (HEADS * HEAD) ** -0.5, 0.15625, ((0, 4),))
    w_up = scatter_about(streams_of[5], (D, FF), D ** -0.5, 0.125, ((1, 4),))
    w_down = scatter_about(streams_of[6], (FF, D), FF ** -0.5, 0.078125, ((0, 4),))
    qk_gains = jnp.clip(jax.random.uniform(streams_of[7], (3, HEAD), jnp.float32, 1.6, 2.4), 1.6, 2.4)
    text_kv = scatter_about(streams_of[8], (2, ITEMS, TXT, HEADS * HEAD), 1.0, 6.0, ((3, 4),))
    timestep = jax.random.randint(streams_of[9], (ITEMS,), 0, STEPS).astype(jnp.int32)
    step_sizes = jnp.clip(jax.random.uniform(streams_of[10], (STEPS,), jnp.float32, -0.6, -0.1), -0.6, -0.1)
    return dict(latent=latent, split_list=split_list, modulation=modulation, w_qkv=w_qkv, w_out=w_out, w_up=w_up, w_down=w_down, qk_gains=qk_gains, text_kv=text_kv, timestep=timestep, step_sizes=step_sizes)


norm_eps = 1e-06

def layer_norm(row_data):
    row_mean = lax.optimization_barrier(jnp.mean(row_data, axis=-1, keepdims=True))
    centred = row_data - row_mean
    variance = lax.optimization_barrier(jnp.mean(centred * centred, axis=-1, keepdims=True))
    return centred * lax.rsqrt(variance + norm_eps)

def head_norm(row_data, gain_row):
    shaped = row_data.reshape(row_data.shape[0], -1, HEAD)
    mean_square = lax.optimization_barrier(jnp.mean(shaped * shaped, axis=-1, keepdims=True))
    return (shaped * lax.rsqrt(mean_square + norm_eps) * gain_row).reshape(row_data.shape)

def one_item(item_rows, item_mods, item_text, w_qkv, w_out, w_up, w_down, qk_gains):
    float_rows = item_rows.astype(jnp.float32)
    normed_one = (layer_norm(float_rows) * (1.0 + item_mods[1]) + item_mods[0]).astype(jnp.bfloat16)
    projected = jnp.einsum('nd,dch->nch', normed_one.astype(jnp.float32), w_qkv.astype(jnp.float32))
    queries = head_norm(projected[:, 0], qk_gains[0]).astype(jnp.bfloat16)
    key_rows = head_norm(projected[:, 1], qk_gains[1]).astype(jnp.bfloat16)
    value_rows = projected[:, 2].astype(jnp.bfloat16)
    text_keys = head_norm(item_text[0].astype(jnp.float32), qk_gains[2]).astype(jnp.bfloat16)
    all_keys = jnp.concatenate([key_rows, text_keys], axis=0).astype(jnp.float32)
    all_values = jnp.concatenate([value_rows, item_text[1]], axis=0).astype(jnp.float32)
    query_count = queries.shape[0]
    heads_all = queries.shape[1] // HEAD
    query_heads = queries.astype(jnp.float32).reshape(query_count, heads_all, HEAD)
    key_heads = all_keys.reshape(-1, heads_all, HEAD)
    value_heads = all_values.reshape(-1, heads_all, HEAD)
    scores = jnp.einsum('qhd,khd->hqk', query_heads, key_heads) * HEAD ** (-0.5)
    weights = jnp.exp(scores)
    totals = lax.optimization_barrier(jnp.sum(weights, axis=-1))
    rounded = lax.optimization_barrier(weights.astype(jnp.bfloat16)).astype(jnp.float32)
    mixed = jnp.einsum('hqk,khd->qhd', rounded, value_heads)
    attended = (mixed / jnp.transpose(totals)[:, :, None]).reshape(query_count, -1).astype(jnp.bfloat16)
    after_attn = float_rows + item_mods[2] * jnp.dot(attended, w_out, preferred_element_type=jnp.float32)
    normed_two = (layer_norm(after_attn) * (1.0 + item_mods[4]) + item_mods[3]).astype(jnp.bfloat16)
    hidden_units = jax.nn.gelu(jnp.dot(normed_two, w_up, preferred_element_type=jnp.float32), approximate=True).astype(jnp.bfloat16)
    return after_attn + item_mods[5] * jnp.dot(hidden_units, w_down, preferred_element_type=jnp.float32)

def reference(latent, split_list, modulation, w_qkv, w_out, w_up, w_down, qk_gains, text_kv, timestep, step_sizes):
    item_a = split_list[:, 0].astype(jnp.int32)
    count_a = split_list[:, 1].astype(jnp.int32)
    item_b = split_list[:, 2].astype(jnp.int32)
    count_b = split_list[:, 3].astype(jnp.int32)
    item_ids = jnp.arange(ITEMS, dtype=jnp.int32)
    held = count_a[:, None] * (item_a[:, None] == item_ids[None, :]).astype(jnp.int32) + count_b[:, None] * (item_b[:, None] == item_ids[None, :]).astype(jnp.int32)
    before = jnp.cumsum(held, axis=0, dtype=jnp.int32) - held
    slot_ids = jnp.arange(CAP, dtype=jnp.int32)[None, :]
    in_first = slot_ids < count_a[:, None]
    slot_live = slot_ids < (count_a + count_b)[:, None]
    base_first = jnp.take_along_axis(before, item_a[:, None], axis=1)
    base_second = jnp.take_along_axis(before, item_b[:, None], axis=1) + jnp.where(item_b == item_a, count_a, 0)[:, None]
    item_rank = jnp.where(in_first, base_first + slot_ids, base_second + slot_ids - count_a[:, None])
    slot_item = jnp.where(in_first, item_a[:, None], item_b[:, None])
    target = jnp.where(slot_live, slot_item * IMG + item_rank, ITEMS * IMG).reshape(-1).astype(jnp.int32)
    placed = jnp.zeros((ITEMS * IMG + 1, D), jnp.bfloat16).at[target].set(latent)
    item_rows = placed[:ITEMS * IMG].reshape(ITEMS, IMG, D)
    moved_text = jnp.moveaxis(text_kv, 1, 0)
    velocity = lax.map(lambda packed: one_item(packed[0], packed[1], packed[2], w_qkv, w_out, w_up, w_down, qk_gains), (item_rows, modulation, moved_text))
    velocity = jnp.concatenate([velocity.reshape(ITEMS * IMG, D), jnp.zeros((1, D), jnp.float32)], axis=0)
    slot_velocity = velocity[target]
    step_items = step_sizes[timestep]
    slot_step = jnp.where(slot_live, step_items[slot_item], 0.0).reshape(-1, 1)
    next_rows = latent.astype(jnp.float32) + slot_step * slot_velocity
    return jnp.where(slot_live.reshape(-1, 1), next_rows, 0.0).astype(jnp.bfloat16)
```

```python
import functools

import jax
import jax.numpy as jnp
from jax import lax
from jax.experimental import pallas as pl
from jax.experimental.pallas import tpu as pltpu
from jax.sharding import PartitionSpec as P

HEAD = 64
IMG = 1024
norm_eps = 1e-06
MESH = pl.DeviceIdType.MESH
f32 = jnp.float32
bf16 = jnp.bfloat16


def layer_norm(rows):
    mean = jnp.mean(rows, axis=-1, keepdims=True)
    centred = rows - mean
    variance = jnp.mean(centred * centred, axis=-1, keepdims=True)
    return centred * lax.rsqrt(variance + norm_eps)


def head_norm(rows, gain):
    mean_square = jnp.mean(rows * rows, axis=0, keepdims=True)
    return rows * lax.rsqrt(mean_square + norm_eps) * gain


def column_chunks(width, step):
    start = 0
    while start < width:
        size = min(step, width - start)
        yield start, size
        start += size


def kernel(
    n, nz, txt,
    lat_ref, split_ref, mod_ref, gain_ref, text_ref, wq_hbm, wo_hbm, wu_hbm, wd_hbm,
    out_ref,
    wq, wo, wu, wd, split_all, t_ref, recv_a, m_ref, e_ref, sel, x_t, q_t, kv_t, q_all, kv_all,
    att_snd, att_t, part_t, recv_e, ga_t, mid_t, recv_g, fin_t, recv_f, res, recv_i,
    w_sem, send_sem, recv_sem,
):
    p = lax.axis_index("patch")
    m = lax.axis_index("mlp")
    share, cap = lat_ref.shape
    half = share // 2
    comp = sel.shape[2]
    width = x_t.shape[0]
    group = IMG // comp
    cols = q_t.shape[0]
    hcols = cols // 2
    heads_half = hcols // HEAD
    c = lax.rem(p, 2)
    pair = p // 2
    sib = p + 1 - 2 * c
    gbase = (p // group) * group
    gpos = p - gbase

    def al(value, unit):
        return pl.multiple_of(value, unit)

    weights = [(wq_hbm, wq), (wo_hbm, wo), (wu_hbm, wu), (wd_hbm, wd)]
    loads = [pltpu.make_async_copy(a, b, w_sem.at[i]) for i, (a, b) in enumerate(weights)]
    for load in loads:
        load.start()

    barrier = pltpu.get_barrier_semaphore()
    for o in range(1, n):
        pl.semaphore_signal(barrier, inc=1, device_id=(lax.rem(p + o, n), m), device_id_type=MESH)
    for o in range(1, nz):
        for q in (p, sib):
            pl.semaphore_signal(barrier, inc=1, device_id=(q, lax.rem(m + o, nz)), device_id_type=MESH)
    pl.semaphore_wait(barrier, n - 1 + 2 * (nz - 1))

    sends = []
    counter = [0]
    rbase = {}
    spot = 0
    for name, count in (
        ("split", n), ("a", n), ("b", 2 * nz), ("q", 1), ("kv", group), ("d", 1),
        ("e", nz), ("f", nz), ("g", nz), ("h", n), ("i", 1),
    ):
        rbase[name] = spot
        spot += count

    def push(src, dst, name, slot, device):
        copy = pltpu.make_async_remote_copy(
            src_ref=src, dst_ref=dst, send_sem=send_sem.at[counter[0]],
            recv_sem=recv_sem.at[rbase[name] + slot], device_id=device, device_id_type=MESH,
        )
        counter[0] += 1
        copy.start()
        sends.append(copy)

    def arrived(dst, name, slot):
        pltpu.make_async_remote_copy(
            src_ref=dst, dst_ref=dst, send_sem=send_sem.at[0],
            recv_sem=recv_sem.at[rbase[name] + slot], device_id=(sib, m), device_id_type=MESH,
        ).wait_recv()

    for o in range(1, n):
        d = lax.rem(p + o, n)
        push(split_ref, split_all.at[pl.ds(al(p * 8, 8), 8), :], "split", p, (d, m))
    for o in range(1, n):
        d = lax.rem(p + o, n)
        push(
            lat_ref.at[pl.ds(al(lax.rem(d, 2) * half, 16), half), :],
            recv_a.at[:, pl.ds(al(p * cap, 128), cap)], "a", p, (d, m),
        )
    split_all[pl.ds(al(p * 8, 8), 8), :] = split_ref[...]
    recv_a[:, pl.ds(al(p * cap, 128), cap)] = lat_ref[pl.ds(al(c * half, 16), half), :]
    for o in range(1, n):
        s = lax.rem(p + o, n)
        arrived(split_all.at[pl.ds(al(s * 8, 8), 8), :], "split", s)

    info = split_all[...]
    rows8 = info.shape[0]
    item_a, count_a = info[:, 0:1], info[:, 1:2]
    item_b, count_b = info[:, 2:3], info[:, 3:4]
    lane = lax.broadcasted_iota(jnp.int32, (rows8, 128), 1).astype(f32)
    held = jnp.where(item_a == lane, count_a, 0.0) + jnp.where(item_b == lane, count_b, 0.0)
    row_i = lax.broadcasted_iota(jnp.int32, (rows8, rows8), 0)
    row_k = lax.broadcasted_iota(jnp.int32, (rows8, rows8), 1)
    lower = jnp.where((row_k % 8 == 0) & (row_k // 8 < row_i // 8), 1.0, 0.0)
    before = jnp.dot(lower.astype(bf16), held.astype(bf16), preferred_element_type=f32)
    base_a = jnp.sum(jnp.where(item_a == lane, before, 0.0), axis=1, keepdims=True)
    base_b = jnp.sum(jnp.where(item_b == lane, before, 0.0), axis=1, keepdims=True)
    base_b = base_b + jnp.where(item_b == item_a, count_a, 0.0)
    slot = lax.broadcasted_iota(jnp.int32, (rows8, cap), 1).astype(f32)
    t_ref[...] = jnp.where(
        slot < count_a,
        item_a * IMG + base_a + slot,
        jnp.where(slot < count_a + count_b, item_b * IMG + base_b + slot - count_a, -1.0),
    )
    want = (lax.broadcasted_iota(jnp.int32, (2 * comp, cap), 0) + pair * (2 * comp)).astype(f32)
    for s in range(n):
        m_ref[:, s * cap:(s + 1) * cap] = jnp.where(
            t_ref[s * 8:s * 8 + 1, :] == want, 1.0, 0.0
        ).astype(bf16)
    for k in range(2):
        mine = t_ref[pl.ds(al((2 * pair + k) * 8, 8), 8), :][0:1, :]
        for s in range(n):
            rows = (lax.broadcasted_iota(jnp.int32, (comp, cap), 0) + s * comp).astype(f32)
            e_ref[s * comp:(s + 1) * comp, k * cap:(k + 1) * cap] = jnp.where(
                mine == rows, 1.0, 0.0
            ).astype(bf16)
    for o in range(1, n):
        s = lax.rem(p + o, n)
        arrived(recv_a.at[:, pl.ds(al(s * cap, 128), cap)], "a", s)
    chosen = lax.dot_general(
        recv_a[...], m_ref[...], (((1,), (1,)), ((), ())), preferred_element_type=f32
    ).astype(bf16)
    sel[0] = chosen[:, :comp]
    sel[1] = chosen[:, comp:]

    def x_rows(z, core):
        return pl.ds(al(z * share + core * half, 16), half)

    for o in range(1, nz):
        z = lax.rem(m + o, nz)
        for k in range(2):
            push(sel.at[k], x_t.at[x_rows(m, c), :], "b", 2 * m + c, (2 * pair + k, z))
    push(sel.at[1 - c], x_t.at[x_rows(m, c), :], "b", 2 * m + c, (sib, m))
    x_t[x_rows(m, c), :] = sel[c]
    arrived(x_t.at[x_rows(m, 1 - c), :], "b", 2 * m + 1 - c)
    for o in range(1, nz):
        z = lax.rem(m + o, nz)
        for k in range(2):
            arrived(x_t.at[x_rows(z, k), :], "b", 2 * z + k)
    x_all = x_t[...].astype(f32).T
    normed = (layer_norm(x_all) * (1.0 + mod_ref[1:2, :]) + mod_ref[0:1, :]).astype(bf16)
    loads[0].wait()
    for j, (gain_col, scale) in enumerate(((1, 1.0), (None, 1.0), (0, HEAD ** -0.5))):
        which = (1, 2, 0)[j]
        proj = jnp.dot(normed, wq[which], preferred_element_type=f32).T
        for h in range(cols // HEAD):
            rows = proj[h * HEAD:(h + 1) * HEAD]
            if gain_col is not None:
                rows = head_norm(rows, gain_ref[:, gain_col:gain_col + 1]) * scale
            if which == 0:
                q_t[h * HEAD:(h + 1) * HEAD, :] = rows.astype(bf16)
            else:
                kv_t[which - 1, h * HEAD:(h + 1) * HEAD, :] = rows.astype(bf16)
        if which == 2:
            for o in range(1, group):
                pos = lax.rem(gpos + o, group)
                push(
                    kv_t.at[:, pl.ds(al(lax.rem(pos, 2) * hcols, 16), hcols), :],
                    kv_all.at[:, :, pl.ds(al(gpos * comp, 128), comp)], "kv", gpos, (gbase + pos, m),
                )
            kv_all[:, :, pl.ds(al(gpos * comp, 128), comp)] = kv_t[:, pl.ds(al(c * hcols, 16), hcols), :]
    push(
        q_t.at[pl.ds(al((1 - c) * hcols, 16), hcols), :],
        q_all.at[:, pl.ds(al(c * comp, 128), comp)], "q", 0, (sib, m),
    )
    q_all[:, pl.ds(al(c * comp, 128), comp)] = q_t[pl.ds(al(c * hcols, 16), hcols), :]

    text_pad = text_ref.shape[2]
    text_k = text_ref[0, pl.ds(al(c * hcols, 16), hcols), :].astype(f32)
    text_v = text_ref[1, pl.ds(al(c * hcols, 16), hcols), :]
    arrived(q_all.at[:, pl.ds(al((1 - c) * comp, 128), comp)], "q", 0)
    live_text = lax.broadcasted_iota(jnp.int32, (text_pad, 2 * comp), 0) < txt
    numer, denom = [], []
    for h in range(heads_half):
        hs = slice(h * HEAD, (h + 1) * HEAD)
        keys = head_norm(text_k[hs], gain_ref[:, 2:3]).T.astype(bf16)
        scores = jnp.dot(keys, q_all[hs, :], preferred_element_type=f32)
        weights_t = jnp.where(live_text, jnp.exp(scores), 0.0)
        denom.append(jnp.sum(weights_t, axis=0, keepdims=True))
        numer.append(jnp.dot(text_v[hs], weights_t.astype(bf16), preferred_element_type=f32))
    for o in range(1, group):
        pos = lax.rem(gpos + o, group)
        arrived(kv_all.at[:, :, pl.ds(al(pos * comp, 128), comp)], "kv", pos)
    for h in range(heads_half):
        hs = slice(h * HEAD, (h + 1) * HEAD)
        keys = kv_all[0, hs, :].astype(f32).T.astype(bf16)
        weights_t = jnp.exp(jnp.dot(keys, q_all[hs, :], preferred_element_type=f32))
        total = denom[h] + jnp.sum(weights_t, axis=0, keepdims=True)
        mixed = numer[h] + jnp.dot(
            kv_all[1, hs, :], weights_t.astype(bf16), preferred_element_type=f32
        )
        attended = (mixed / total).astype(bf16)
        att_snd[0, hs, :] = attended[:, :comp]
        att_snd[1, hs, :] = attended[:, comp:]
    push(att_snd.at[1 - c], att_t.at[pl.ds(al(c * hcols, 16), hcols), :], "d", 0, (sib, m))
    att_t[pl.ds(al(c * hcols, 16), hcols), :] = att_snd[c]
    loads[1].wait()
    arrived(att_t.at[pl.ds(al((1 - c) * hcols, 16), hcols), :], "d", 0)

    def reduce_over_mlp(lhs, w_ref, gate_row, buf, recv, name):
        sent = 0
        for start, size in column_chunks(width, 256):
            block = jnp.dot(lhs, w_ref[:, start:start + size], preferred_element_type=f32)
            block = block * mod_ref[gate_row:gate_row + 1, start:start + size]
            buf[start:start + size, :] = block.T.astype(bf16)
            while sent < nz and (sent + 1) * share <= start + size:
                send_to(buf, recv, name, sent)
                sent += 1
        for o in range(1, nz):
            z = lax.rem(m + o, nz)
            arrived(recv.at[z], name, z)
        total = buf[pl.ds(al(m * share, 16), share), :].astype(f32)
        for o in range(1, nz):
            total = total + recv[lax.rem(m + o, nz)].astype(f32)
        return total

    waits = []

    def send_to(buf, recv, name, z):
        index = counter[0]
        counter[0] += 1
        copy = pltpu.make_async_remote_copy(
            src_ref=buf.at[z * share:(z + 1) * share, :], dst_ref=recv.at[m],
            send_sem=send_sem.at[index], recv_sem=recv_sem.at[rbase[name] + m],
            device_id=(p, z), device_id_type=MESH,
        )

        @pl.when(m != z)
        def _():
            copy.start()

        waits.append((z, copy))

    attended = att_t[...].astype(f32).T.astype(bf16)
    ga = reduce_over_mlp(attended, wo, 2, part_t, recv_e, "e")
    ga_low = ga.astype(bf16)
    ga_rows = pl.ds(al(m * share, 16), share)
    ga_t[ga_rows, :] = ga_low
    for o in range(1, nz):
        push(ga_t.at[ga_rows, :], ga_t.at[ga_rows, :], "f", m, (p, lax.rem(m + o, nz)))
    loads[2].wait()
    for o in range(1, nz):
        z = lax.rem(m + o, nz)
        arrived(ga_t.at[pl.ds(al(z * share, 16), share), :], "f", z)
    after = x_all + ga_t[...].astype(f32).T
    normed_two = (layer_norm(after) * (1.0 + mod_ref[4:5, :]) + mod_ref[3:4, :]).astype(bf16)
    hidden = []
    for start, size in column_chunks(wu.shape[1], 256):
        up = jnp.dot(normed_two, wu[:, start:start + size], preferred_element_type=f32)
        hidden.append(jax.nn.gelu(up, approximate=True).astype(bf16))
    hidden = jnp.concatenate(hidden, axis=1)
    loads[3].wait()
    gm = reduce_over_mlp(hidden, wd, 5, mid_t, recv_g, "g")
    x_own = x_t[ga_rows, :].astype(f32)
    step = mod_ref[6:7, :comp]
    fin_t[...] = (x_own + step * (x_own + ga + gm)).astype(bf16)

    for o in range(1, n):
        d = lax.rem(p + o, n)
        push(
            fin_t.at[pl.ds(al(lax.rem(d, 2) * half, 16), half), :],
            recv_f.at[:, pl.ds(al(p * comp, 128), comp)], "h", p, (d, m),
        )
    recv_f[:, pl.ds(al(p * comp, 128), comp)] = fin_t[pl.ds(al(c * half, 16), half), :]
    for o in range(1, n):
        s = lax.rem(p + o, n)
        arrived(recv_f.at[:, pl.ds(al(s * comp, 128), comp)], "h", s)
    spread = jnp.dot(recv_f[...], e_ref[...], preferred_element_type=f32).astype(bf16)
    res[0] = spread[:, :cap]
    res[1] = spread[:, cap:]
    push(res.at[1 - c], recv_i, "i", 0, (sib, m))
    out_ref[pl.ds(al(c * half, 16), half), :] = res[c]
    arrived(recv_i, "i", 0)
    out_ref[pl.ds(al((1 - c) * half, 16), half), :] = recv_i[...]
    for copy in sends:
        copy.wait_send()
    for z, copy in waits:
        @pl.when(m != z)
        def _():
            copy.wait_send()


def body(
    n, nz,
    latent, split_list, modulation, w_qkv, w_out, w_up, w_down, qk_gains, text_kv, timestep, step_sizes,
):
    cap, share = latent.shape
    width = share * nz
    items = modulation.shape[0]
    comp = items * IMG // n
    group = IMG // comp
    cols = w_out.shape[0]
    hcols = cols // 2
    hidden = w_up.shape[1]
    txt = text_kv.shape[2]
    text_pad = -(-txt // 128) * 128
    half = share // 2

    item = lax.axis_index("patch") // group
    mods = lax.dynamic_index_in_dim(modulation, item, 0, keepdims=False)
    step = step_sizes[lax.dynamic_index_in_dim(timestep, item, 0, keepdims=False)]
    mods = jnp.concatenate([mods, jnp.broadcast_to(step, (2, width))], axis=0)
    split = jnp.broadcast_to(jnp.pad(split_list.astype(f32), ((0, 0), (0, 124))), (8, 128))
    gains = jnp.pad(qk_gains.T, ((0, 0), (0, 125)))
    text = lax.dynamic_index_in_dim(text_kv, item, 1, keepdims=False)
    text = jnp.pad(jnp.swapaxes(text, 1, 2), ((0, 0), (0, 0), (0, text_pad - txt)))

    vmem = pl.BlockSpec(memory_space=pltpu.VMEM)
    hbm = pl.BlockSpec(memory_space=pl.ANY)
    recv_count = 2 * n + 2 * nz + 1 + group + 1 + 3 * nz + n + 1
    send_count = 3 * (n - 1) + 2 * (nz - 1) + 1 + group - 1 + 1 + 1 + 2 * nz + nz - 1 + 1
    out = pl.pallas_call(
        functools.partial(kernel, n, nz, txt),
        out_shape=jax.ShapeDtypeStruct((share, cap), bf16),
        in_specs=[vmem] * 5 + [hbm] * 4,
        out_specs=vmem,
        scratch_shapes=[
            pltpu.VMEM((3, width, cols), bf16),
            pltpu.VMEM((cols, width), bf16),
            pltpu.VMEM((width, hidden), bf16),
            pltpu.VMEM((hidden, width), bf16),
            pltpu.VMEM((n * 8, 128), f32),
            pltpu.VMEM((n * 8, cap), f32),
            pltpu.VMEM((half, n * cap), bf16),
            pltpu.VMEM((2 * comp, n * cap), bf16),
            pltpu.VMEM((n * comp, 2 * cap), bf16),
            pltpu.VMEM((2, half, comp), bf16),
            pltpu.VMEM((width, comp), bf16),
            pltpu.VMEM((cols, comp), bf16),
            pltpu.VMEM((2, cols, comp), bf16),
            pltpu.VMEM((hcols, 2 * comp), bf16),
            pltpu.VMEM((2, hcols, group * comp), bf16),
            pltpu.VMEM((2, hcols, comp), bf16),
            pltpu.VMEM((cols, comp), bf16),
            pltpu.VMEM((width, comp), bf16),
            pltpu.VMEM((nz, share, comp), bf16),
            pltpu.VMEM((width, comp), bf16),
            pltpu.VMEM((width, comp), bf16),
            pltpu.VMEM((nz, share, comp), bf16),
            pltpu.VMEM((share, comp), bf16),
            pltpu.VMEM((half, n * comp), bf16),
            pltpu.VMEM((2, half, cap), bf16),
            pltpu.VMEM((half, cap), bf16),
            pltpu.SemaphoreType.DMA((4,)),
            pltpu.SemaphoreType.DMA((send_count,)),
            pltpu.SemaphoreType.DMA((recv_count,)),
        ],
        compiler_params=pltpu.CompilerParams(
            collective_id=0, has_side_effects=True, vmem_limit_bytes=58 * 1024 * 1024
        ),
    )(latent.T, split, mods, gains, text, jnp.swapaxes(w_qkv, 0, 1), w_out, w_up, w_down)
    return out.T


def solution(mesh):
    return jax.shard_map(
        functools.partial(body, mesh.shape["patch"], mesh.shape["mlp"]),
        mesh=mesh,
        in_specs=(
            P("patch", "mlp"),
            P("patch", None),
            P(),
            P(None, None, "mlp"),
            P("mlp", None),
            P(None, "mlp"),
            P("mlp", None),
            P(),
            P(None, None, None, "mlp"),
            P(),
            P(),
        ),
        out_specs=P("patch", "mlp"),
        check_vma=False,
    )
```

```python
import functools

import jax
import jax.numpy as jnp
from jax import lax
from jax.experimental import pallas as pl
from jax.experimental.pallas import tpu as pltpu
from jax.sharding import PartitionSpec as P

HEAD = 64
IMG = 1024
norm_eps = 1e-06
MESH = pl.DeviceIdType.MESH
f32 = jnp.float32
bf16 = jnp.bfloat16


def layer_norm(rows):
    mean = jnp.mean(rows, axis=-1, keepdims=True)
    centred = rows - mean
    variance = jnp.mean(centred * centred, axis=-1, keepdims=True)
    return centred * lax.rsqrt(variance + norm_eps)


def head_norm(rows, gain):
    mean_square = jnp.mean(rows * rows, axis=0, keepdims=True)
    return rows * lax.rsqrt(mean_square + norm_eps) * gain


def column_chunks(width, step):
    start = 0
    while start < width:
        size = min(step, width - start)
        yield start, size
        start += size


def kernel(
    n, nz, txt,
    lat_ref, list_ref, mods_ref, gains_ref, texts_ref, time_ref, steps_ref, wq_hbm, wo_hbm, wu_hbm, wd_hbm,
    out_ref,
    wq, wo, wu, wd, split_ref, gain_pad, text_rows, text_t, split_all, t_ref, recv_a, m_ref, e_ref, sel, x_t, q_t, kv_t, q_all, kv_all,
    att_snd, att_t, part_t, recv_e, ga_t, ga_own, mid_t, recv_g, fin_t, recv_f, res, recv_i,
    w_sem, send_sem, recv_sem,
):
    p = lax.axis_index("patch")
    m = lax.axis_index("mlp")
    share, cap = lat_ref.shape
    half = share // 2
    comp = sel.shape[2]
    width = x_t.shape[0]
    group = IMG // comp
    cols = q_t.shape[0]
    hcols = cols // 2
    heads_half = hcols // HEAD
    c = lax.rem(p, 2)
    pair = p // 2
    sib = p + 1 - 2 * c
    gbase = (p // group) * group
    gpos = p - gbase

    def al(value, unit):
        return pl.multiple_of(value, unit)

    weights = [(wq_hbm, wq), (wo_hbm, wo), (wu_hbm, wu), (wd_hbm, wd)]
    loads = [pltpu.make_async_copy(a, b, w_sem.at[i]) for i, (a, b) in enumerate(weights)]
    for load in loads:
        load.start()

    item = p // group
    lane8 = lax.broadcasted_iota(jnp.int32, (8, 128), 1)
    listed = jnp.zeros((8, 128), jnp.int32)
    for k in range(4):
        listed = jnp.where(lane8 == k, list_ref[0, k], listed)
    split_ref[...] = listed.astype(f32)
    step = steps_ref[time_ref[item]]

    def mod(row):
        return mods_ref[item, row:row + 1, :]

    barrier = pltpu.get_barrier_semaphore()
    for o in range(1, n):
        pl.semaphore_signal(barrier, inc=1, device_id=(lax.rem(p + o, n), m), device_id_type=MESH)
    for o in range(1, nz):
        for q in (p, sib):
            pl.semaphore_signal(barrier, inc=1, device_id=(q, lax.rem(m + o, nz)), device_id_type=MESH)
    pl.semaphore_wait(barrier, n - 1 + 2 * (nz - 1))

    sends = []
    counter = [0]
    rbase = {}
    spot = 0
    for name, count in (
        ("split", n), ("a", 2 * n), ("b", 4 * nz), ("q", 1), ("kv", group), ("d", 1),
        ("e", 2 * nz), ("f", 2 * nz), ("g", 2 * nz), ("h", n), ("i", 1),
    ):
        rbase[name] = spot
        spot += count

    def push(src, dst, name, slot, device):
        copy = pltpu.make_async_remote_copy(
            src_ref=src, dst_ref=dst, send_sem=send_sem.at[counter[0]],
            recv_sem=recv_sem.at[rbase[name] + slot], device_id=device, device_id_type=MESH,
        )
        counter[0] += 1
        copy.start()
        sends.append(copy)

    def arrived(dst, name, slot):
        pltpu.make_async_remote_copy(
            src_ref=dst, dst_ref=dst, send_sem=send_sem.at[0],
            recv_sem=recv_sem.at[rbase[name] + slot], device_id=(sib, m), device_id_type=MESH,
        ).wait_recv()

    for o in range(1, n):
        d = lax.rem(p + o, n)
        push(split_ref, split_all.at[pl.ds(al(p * 8, 8), 8), :], "split", p, (d, m))
    first = -(-half // 32) * 16
    parts = ((0, first), (first, half - first))
    for k, (start, size) in enumerate(parts):
        for o in range(1, n):
            d = lax.rem(p + o, n)
            push(
                lat_ref.at[pl.ds(al(lax.rem(d, 2) * half + start, 16), size), :],
                recv_a.at[start:start + size, pl.ds(al(p * cap, 128), cap)], "a", 2 * p + k, (d, m),
            )
    split_all[pl.ds(al(p * 8, 8), 8), :] = split_ref[...]
    recv_a[:, pl.ds(al(p * cap, 128), cap)] = lat_ref[pl.ds(al(c * half, 16), half), :]
    for o in range(1, n):
        s = lax.rem(p + o, n)
        arrived(split_all.at[pl.ds(al(s * 8, 8), 8), :], "split", s)

    info = split_all[...]
    rows8 = info.shape[0]
    item_a, count_a = info[:, 0:1], info[:, 1:2]
    item_b, count_b = info[:, 2:3], info[:, 3:4]
    lane = lax.broadcasted_iota(jnp.int32, (rows8, 128), 1).astype(f32)
    held = jnp.where(item_a == lane, count_a, 0.0) + jnp.where(item_b == lane, count_b, 0.0)
    row_i = lax.broadcasted_iota(jnp.int32, (rows8, rows8), 0)
    row_k = lax.broadcasted_iota(jnp.int32, (rows8, rows8), 1)
    lower = jnp.where((row_k % 8 == 0) & (row_k // 8 < row_i // 8), 1.0, 0.0)
    before = jnp.dot(lower.astype(bf16), held.astype(bf16), preferred_element_type=f32)
    base_a = jnp.sum(jnp.where(item_a == lane, before, 0.0), axis=1, keepdims=True)
    base_b = jnp.sum(jnp.where(item_b == lane, before, 0.0), axis=1, keepdims=True)
    base_b = base_b + jnp.where(item_b == item_a, count_a, 0.0)
    slot = lax.broadcasted_iota(jnp.int32, (rows8, cap), 1).astype(f32)
    t_ref[...] = jnp.where(
        slot < count_a,
        item_a * IMG + base_a + slot,
        jnp.where(slot < count_a + count_b, item_b * IMG + base_b + slot - count_a, -1.0),
    )
    want = (lax.broadcasted_iota(jnp.int32, (2 * comp, cap), 0) + pair * (2 * comp)).astype(f32)
    for s in range(n):
        m_ref[:, s * cap:(s + 1) * cap] = jnp.where(
            t_ref[s * 8:s * 8 + 1, :] == want, 1.0, 0.0
        ).astype(bf16)
    for k in range(2):
        mine = t_ref[pl.ds(al((2 * pair + k) * 8, 8), 8), :][0:1, :]
        for s in range(n):
            rows = (lax.broadcasted_iota(jnp.int32, (comp, cap), 0) + s * comp).astype(f32)
            e_ref[s * comp:(s + 1) * comp, k * cap:(k + 1) * cap] = jnp.where(
                mine == rows, 1.0, 0.0
            ).astype(bf16)
    gain_pad[...] = jnp.zeros_like(gain_pad)
    gain_pad[0:gains_ref.shape[0], 0:HEAD] = gains_ref[...]
    gain_ref = gain_pad[...].T[:HEAD, :]
    text_rows[...] = jnp.zeros_like(text_rows)
    for k in range(2):
        text_rows[0:txt, :] = texts_ref[k, item].astype(f32)
        text_t[k] = text_rows[...].T.astype(bf16)

    def x_rows(z, core, part):
        return pl.ds(al(z * share + core * half + part[0], 16), part[1])

    for k, (start, size) in enumerate(parts):
        for o in range(1, n):
            s = lax.rem(p + o, n)
            arrived(recv_a.at[start:start + size, pl.ds(al(s * cap, 128), cap)], "a", 2 * s + k)
        chosen = lax.dot_general(
            recv_a[start:start + size, :], m_ref[...], (((1,), (1,)), ((), ())),
            preferred_element_type=f32,
        ).astype(bf16)
        sel[0, start:start + size, :] = chosen[:, :comp]
        sel[1, start:start + size, :] = chosen[:, comp:]
        mine = x_rows(m, c, (start, size))
        spot_b = 2 * (2 * m + c) + k
        for o in range(1, nz):
            z = lax.rem(m + o, nz)
            for q in range(2):
                push(sel.at[q, start:start + size, :], x_t.at[mine, :], "b", spot_b, (2 * pair + q, z))
        push(sel.at[1 - c, start:start + size, :], x_t.at[mine, :], "b", spot_b, (sib, m))
        x_t[mine, :] = sel[c, start:start + size, :]
    for k, part in enumerate(parts):
        arrived(x_t.at[x_rows(m, 1 - c, part), :], "b", 2 * (2 * m + 1 - c) + k)
        for o in range(1, nz):
            z = lax.rem(m + o, nz)
            for q in range(2):
                arrived(x_t.at[x_rows(z, q, part), :], "b", 2 * (2 * z + q) + k)
    x_all = x_t[...].astype(f32).T
    normed = (layer_norm(x_all) * (1.0 + mod(1)) + mod(0)).astype(bf16)
    loads[0].wait()
    for j, (gain_col, scale) in enumerate(((1, 1.0), (None, 1.0), (0, HEAD ** -0.5))):
        which = (1, 2, 0)[j]
        proj = jnp.dot(normed, wq[which], preferred_element_type=f32).T
        for h in range(cols // HEAD):
            rows = proj[h * HEAD:(h + 1) * HEAD]
            if gain_col is not None:
                rows = head_norm(rows, gain_ref[:, gain_col:gain_col + 1]) * scale
            if which == 0:
                q_t[h * HEAD:(h + 1) * HEAD, :] = rows.astype(bf16)
            else:
                kv_t[which - 1, h * HEAD:(h + 1) * HEAD, :] = rows.astype(bf16)
        if which == 2:
            for o in range(1, group):
                pos = lax.rem(gpos + o, group)
                push(
                    kv_t.at[:, pl.ds(al(lax.rem(pos, 2) * hcols, 16), hcols), :],
                    kv_all.at[:, :, pl.ds(al(gpos * comp, 128), comp)], "kv", gpos, (gbase + pos, m),
                )
            kv_all[:, :, pl.ds(al(gpos * comp, 128), comp)] = kv_t[:, pl.ds(al(c * hcols, 16), hcols), :]
    push(
        q_t.at[pl.ds(al((1 - c) * hcols, 16), hcols), :],
        q_all.at[:, pl.ds(al(c * comp, 128), comp)], "q", 0, (sib, m),
    )
    q_all[:, pl.ds(al(c * comp, 128), comp)] = q_t[pl.ds(al(c * hcols, 16), hcols), :]

    text_pad = text_t.shape[2]
    text_k = text_t[0, pl.ds(al(c * hcols, 16), hcols), :].astype(f32)
    text_v = text_t[1, pl.ds(al(c * hcols, 16), hcols), :]
    arrived(q_all.at[:, pl.ds(al((1 - c) * comp, 128), comp)], "q", 0)
    live_text = lax.broadcasted_iota(jnp.int32, (text_pad, 2 * comp), 0) < txt
    numer, denom = [], []
    for h in range(heads_half):
        hs = slice(h * HEAD, (h + 1) * HEAD)
        keys = head_norm(text_k[hs], gain_ref[:, 2:3]).T.astype(bf16)
        scores = jnp.dot(keys, q_all[hs, :], preferred_element_type=f32)
        weights_t = jnp.where(live_text, jnp.exp(scores), 0.0)
        denom.append(jnp.sum(weights_t, axis=0, keepdims=True))
        numer.append(jnp.dot(text_v[hs], weights_t.astype(bf16), preferred_element_type=f32))
    for o in range(1, group):
        pos = lax.rem(gpos + o, group)
        arrived(kv_all.at[:, :, pl.ds(al(pos * comp, 128), comp)], "kv", pos)
    for h in range(heads_half):
        hs = slice(h * HEAD, (h + 1) * HEAD)
        keys = kv_all[0, hs, :].astype(f32).T.astype(bf16)
        weights_t = jnp.exp(jnp.dot(keys, q_all[hs, :], preferred_element_type=f32))
        total = denom[h] + jnp.sum(weights_t, axis=0, keepdims=True)
        mixed = numer[h] + jnp.dot(
            kv_all[1, hs, :], weights_t.astype(bf16), preferred_element_type=f32
        )
        attended = (mixed / total).astype(bf16)
        att_snd[0, hs, :] = attended[:, :comp]
        att_snd[1, hs, :] = attended[:, comp:]
    push(att_snd.at[1 - c], att_t.at[pl.ds(al(c * hcols, 16), hcols), :], "d", 0, (sib, m))
    att_t[pl.ds(al(c * hcols, 16), hcols), :] = att_snd[c]
    loads[1].wait()
    arrived(att_t.at[pl.ds(al((1 - c) * hcols, 16), hcols), :], "d", 0)

    halves = ((0, half), (half, share - half))
    line_sends = []

    def scatter_over_mlp(lhs, w_ref, gate_row, buf, recv, name, early):
        sent = 0
        for start, size in column_chunks(width, 256):
            block = jnp.dot(lhs, w_ref[:, start:start + size], preferred_element_type=f32)
            block = block * mods_ref[item, gate_row:gate_row + 1, start:start + size]
            buf[start:start + size, :] = block.T.astype(bf16)
            while early and sent < nz and (sent + 1) * share <= start + size:
                for k, part in enumerate(halves):
                    index = counter[0]
                    counter[0] += 1
                    copy = pltpu.make_async_remote_copy(
                        src_ref=buf.at[sent * share + part[0]:sent * share + part[0] + part[1], :],
                        dst_ref=recv.at[m, part[0]:part[0] + part[1], :],
                        send_sem=send_sem.at[index], recv_sem=recv_sem.at[rbase[name] + 2 * m + k],
                        device_id=(p, sent), device_id_type=MESH,
                    )

                    @pl.when(m != sent)
                    def _():
                        copy.start()
                    line_sends.append((m != sent, copy))
                sent += 1
        if not early:
            for k, part in enumerate(halves):
                for o in range(1, nz):
                    z = lax.rem(m + o, nz)
                    push(
                        buf.at[pl.ds(al(z * share + part[0], 16), part[1]), :],
                        recv.at[m, part[0]:part[0] + part[1], :], name, 2 * m + k, (p, z),
                    )

    def summed(buf, recv, name, k):
        start, size = halves[k]
        for o in range(1, nz):
            z = lax.rem(m + o, nz)
            arrived(recv.at[z, start:start + size, :], name, 2 * z + k)
        total = buf[pl.ds(al(m * share + start, 16), size), :].astype(f32)
        for o in range(1, nz):
            total = total + recv[lax.rem(m + o, nz), start:start + size, :].astype(f32)
        return total

    def line_hop(buf, name, s, k):
        start, size = halves[k]
        for way in (1, -1):
            block = m - way * s
            held_here = (block >= 0) & (block < nz)
            safe = lax.rem(block + nz, nz)
            index = counter[0]
            counter[0] += 1
            ref = buf.at[pl.ds(al(safe * share + start, 16), size), :]
            copy = pltpu.make_async_remote_copy(
                src_ref=ref, dst_ref=ref, send_sem=send_sem.at[index],
                recv_sem=recv_sem.at[rbase[name] + 2 * safe + k],
                device_id=(p, lax.rem(m + way + nz, nz)), device_id_type=MESH,
            )
            if s > 0:
                @pl.when(held_here)
                def _():
                    copy.wait_recv()
            if s < nz - 1:
                go = held_here & (m + way >= 0) & (m + way < nz)

                @pl.when(go)
                def _():
                    copy.start()
                line_sends.append((go, copy))

    attended = att_t[...].astype(f32).T.astype(bf16)
    scatter_over_mlp(attended, wo, 2, part_t, recv_e, "e", False)
    own_rows = [pl.ds(al(m * share + start, 16), size) for start, size in halves]
    for k in range(2):
        ga = summed(part_t, recv_e, "e", k)
        ga_own[halves[k][0]:halves[k][0] + halves[k][1], :] = ga
        ga_t[own_rows[k], :] = ga.astype(bf16)
        line_hop(ga_t, "f", 0, k)
    loads[2].wait()
    for s in range(1, nz):
        for k in range(2):
            line_hop(ga_t, "f", s, k)
    after = x_all + ga_t[...].astype(f32).T
    normed_two = (layer_norm(after) * (1.0 + mod(4)) + mod(3)).astype(bf16)
    hidden = []
    for start, size in column_chunks(wu.shape[1], 256):
        up = jnp.dot(normed_two, wu[:, start:start + size], preferred_element_type=f32)
        hidden.append(jax.nn.gelu(up, approximate=True).astype(bf16))
    hidden = jnp.concatenate(hidden, axis=1)
    loads[3].wait()
    scatter_over_mlp(hidden, wd, 5, mid_t, recv_g, "g", True)

    for k in range(2):
        gm = summed(mid_t, recv_g, "g", k)
        own = slice(halves[k][0], halves[k][0] + halves[k][1])
        x_own = x_t[own_rows[k], :].astype(f32)
        fin_t[own, :] = (x_own + step * (x_own + ga_own[own, :] + gm)).astype(bf16)
        for o in range(0, n, 2):
            d = lax.rem(pair * 2 + k + o, n)
            index = counter[0]
            counter[0] += 1
            copy = pltpu.make_async_remote_copy(
                src_ref=fin_t.at[own, :], dst_ref=recv_f.at[:, pl.ds(al(p * comp, 128), comp)],
                send_sem=send_sem.at[index], recv_sem=recv_sem.at[rbase["h"] + p],
                device_id=(d, m), device_id_type=MESH,
            )

            @pl.when(d != p)
            def _():
                copy.start()
            line_sends.append((d != p, copy))
    recv_f[:, pl.ds(al(p * comp, 128), comp)] = fin_t[pl.ds(al(c * half, 16), half), :]
    for o in range(1, n):
        s = lax.rem(p + o, n)
        arrived(recv_f.at[:, pl.ds(al(s * comp, 128), comp)], "h", s)
    spread = jnp.dot(recv_f[...], e_ref[...], preferred_element_type=f32).astype(bf16)
    res[0] = spread[:, :cap]
    res[1] = spread[:, cap:]
    push(res.at[1 - c], recv_i, "i", 0, (sib, m))
    out_ref[pl.ds(al(c * half, 16), half), :] = res[c]
    arrived(recv_i, "i", 0)
    out_ref[pl.ds(al((1 - c) * half, 16), half), :] = recv_i[...]
    for copy in sends:
        copy.wait_send()
    for go, copy in line_sends:
        @pl.when(go)
        def _():
            copy.wait_send()


def body(
    n, nz,
    latent, split_list, modulation, w_qkv, w_out, w_up, w_down, qk_gains, text_kv, timestep, step_sizes,
):
    cap, share = latent.shape
    width = share * nz
    items = modulation.shape[0]
    comp = items * IMG // n
    group = IMG // comp
    cols = w_out.shape[0]
    hcols = cols // 2
    hidden = w_up.shape[1]
    txt = text_kv.shape[2]
    text_pad = -(-txt // 128) * 128
    half = share // 2

    vmem = pl.BlockSpec(memory_space=pltpu.VMEM)
    smem = pl.BlockSpec(memory_space=pltpu.SMEM)
    hbm = pl.BlockSpec(memory_space=pl.ANY)
    recv_count = 4 * n + 10 * nz + group + 3
    send_count = 4 * n + 4 * nz + group + 16 * nz + n + 4
    out = pl.pallas_call(
        functools.partial(kernel, n, nz, txt),
        out_shape=jax.ShapeDtypeStruct((share, cap), bf16),
        in_specs=[vmem, smem, vmem, vmem, vmem, smem, smem] + [hbm] * 4,
        out_specs=vmem,
        scratch_shapes=[
            pltpu.VMEM((3, width, cols), bf16),
            pltpu.VMEM((cols, width), bf16),
            pltpu.VMEM((width, hidden), bf16),
            pltpu.VMEM((hidden, width), bf16),
            pltpu.VMEM((8, 128), f32),
            pltpu.VMEM((128, 128), f32),
            pltpu.VMEM((text_pad, cols), f32),
            pltpu.VMEM((2, cols, text_pad), bf16),
            pltpu.VMEM((n * 8, 128), f32),
            pltpu.VMEM((n * 8, cap), f32),
            pltpu.VMEM((half, n * cap), bf16),
            pltpu.VMEM((2 * comp, n * cap), bf16),
            pltpu.VMEM((n * comp, 2 * cap), bf16),
            pltpu.VMEM((2, half, comp), bf16),
            pltpu.VMEM((width, comp), bf16),
            pltpu.VMEM((cols, comp), bf16),
            pltpu.VMEM((2, cols, comp), bf16),
            pltpu.VMEM((hcols, 2 * comp), bf16),
            pltpu.VMEM((2, hcols, group * comp), bf16),
            pltpu.VMEM((2, hcols, comp), bf16),
            pltpu.VMEM((cols, comp), bf16),
            pltpu.VMEM((width, comp), bf16),
            pltpu.VMEM((nz, share, comp), bf16),
            pltpu.VMEM((width, comp), bf16),
            pltpu.VMEM((share, comp), f32),
            pltpu.VMEM((width, comp), bf16),
            pltpu.VMEM((nz, share, comp), bf16),
            pltpu.VMEM((share, comp), bf16),
            pltpu.VMEM((half, n * comp), bf16),
            pltpu.VMEM((2, half, cap), bf16),
            pltpu.VMEM((half, cap), bf16),
            pltpu.SemaphoreType.DMA((4,)),
            pltpu.SemaphoreType.DMA((send_count,)),
            pltpu.SemaphoreType.DMA((recv_count,)),
        ],
        compiler_params=pltpu.CompilerParams(
            collective_id=0, has_side_effects=True, vmem_limit_bytes=58 * 1024 * 1024
        ),
    )(latent.T, split_list, modulation, qk_gains, text_kv, timestep, step_sizes, jnp.swapaxes(w_qkv, 0, 1), w_out, w_up, w_down)
    return out.T


def solution(mesh):
    return jax.shard_map(
        functools.partial(body, mesh.shape["patch"], mesh.shape["mlp"]),
        mesh=mesh,
        in_specs=(
            P("patch", "mlp"),
            P("patch", None),
            P(),
            P(None, None, "mlp"),
            P("mlp", None),
            P(None, "mlp"),
            P("mlp", None),
            P(),
            P(None, None, None, "mlp"),
            P(),
            P(),
        ),
        out_specs=P("patch", "mlp"),
        check_vma=False,
    )
```

```python
import functools

import jax
import jax.numpy as jnp
from jax import lax
from jax.experimental import pallas as pl
from jax.experimental.pallas import tpu as pltpu
from jax.sharding import PartitionSpec as P

HEAD = 64
IMG = 1024
norm_eps = 1e-06
MESH = pl.DeviceIdType.MESH
f32 = jnp.float32
bf16 = jnp.bfloat16


def layer_norm(rows):
    mean = jnp.mean(rows, axis=-1, keepdims=True)
    centred = rows - mean
    variance = jnp.mean(centred * centred, axis=-1, keepdims=True)
    return centred * lax.rsqrt(variance + norm_eps)


def head_norm(rows, gain):
    mean_square = jnp.mean(rows * rows, axis=0, keepdims=True)
    return rows * lax.rsqrt(mean_square + norm_eps) * gain


def column_chunks(width, step):
    start = 0
    while start < width:
        size = min(step, width - start)
        yield start, size
        start += size


def kernel(
    n, nz, txt,
    lat_ref, list_ref, mods_ref, gains_ref, texts_ref, time_ref, steps_ref, wq_hbm, wo_hbm, wu_hbm, wd_hbm,
    out_ref,
    wq, wo, wu, wd, split_ref, gain_pad, text_rows, text_t, split_all, t_ref, recv_a, m_ref, e_ref, sel, x_t, q_t, kv_t, q_all, kv_all,
    att_snd, att_t, part_t, recv_e, ga_t, ga_own, mid_t, recv_g, fin_t, recv_f, res, recv_i,
    w_sem, send_sem, recv_sem,
):
    p = lax.axis_index("patch")
    m = lax.axis_index("mlp")
    share, cap = lat_ref.shape
    half = share // 2
    comp = sel.shape[2]
    width = x_t.shape[0]
    group = IMG // comp
    cols = q_t.shape[0]
    hcols = cols // 2
    heads_half = hcols // HEAD
    c = lax.rem(p, 2)
    pair = p // 2
    sib = p + 1 - 2 * c
    gbase = (p // group) * group
    gpos = p - gbase

    def al(value, unit):
        return pl.multiple_of(value, unit)

    weights = [(wq_hbm, wq), (wo_hbm, wo), (wu_hbm, wu), (wd_hbm, wd)]
    loads = [pltpu.make_async_copy(a, b, w_sem.at[i]) for i, (a, b) in enumerate(weights)]
    for load in loads:
        load.start()

    item = p // group
    lane8 = lax.broadcasted_iota(jnp.int32, (8, 128), 1)
    listed = jnp.zeros((8, 128), jnp.int32)
    for k in range(4):
        listed = jnp.where(lane8 == k, list_ref[0, k], listed)
    split_ref[...] = listed.astype(f32)
    step = steps_ref[time_ref[item]]

    def mod(row):
        return mods_ref[row, item, :, :]

    barrier = pltpu.get_barrier_semaphore()
    for o in range(1, n):
        pl.semaphore_signal(barrier, inc=1, device_id=(lax.rem(p + o, n), m), device_id_type=MESH)
    for o in range(1, nz):
        for q in (p, sib):
            pl.semaphore_signal(barrier, inc=1, device_id=(q, lax.rem(m + o, nz)), device_id_type=MESH)
    pl.semaphore_wait(barrier, n - 1 + 2 * (nz - 1))

    sends = []
    counter = [0]
    rbase = {}
    spot = 0
    for name, count in (
        ("split", n), ("a", 2 * n), ("b", 4 * nz), ("q", 1), ("kv", 2 * group), ("d", 1),
        ("e", 2 * nz), ("f", 2 * nz), ("g", 2 * nz), ("h", n), ("i", 1),
    ):
        rbase[name] = spot
        spot += count

    def push(src, dst, name, slot, device):
        copy = pltpu.make_async_remote_copy(
            src_ref=src, dst_ref=dst, send_sem=send_sem.at[counter[0]],
            recv_sem=recv_sem.at[rbase[name] + slot], device_id=device, device_id_type=MESH,
        )
        counter[0] += 1
        copy.start()
        sends.append(copy)

    def arrived(dst, name, slot):
        pltpu.make_async_remote_copy(
            src_ref=dst, dst_ref=dst, send_sem=send_sem.at[0],
            recv_sem=recv_sem.at[rbase[name] + slot], device_id=(sib, m), device_id_type=MESH,
        ).wait_recv()

    for o in range(1, n):
        d = lax.rem(p + o, n)
        push(split_ref, split_all.at[pl.ds(al(p * 8, 8), 8), :], "split", p, (d, m))
    first = -(-half // 32) * 16
    parts = ((0, first), (first, half - first))
    for k, (start, size) in enumerate(parts):
        for o in range(1, n):
            d = lax.rem(p + o, n)
            push(
                lat_ref.at[pl.ds(al(lax.rem(d, 2) * half + start, 16), size), :],
                recv_a.at[start:start + size, pl.ds(al(p * cap, 128), cap)], "a", 2 * p + k, (d, m),
            )
    split_all[pl.ds(al(p * 8, 8), 8), :] = split_ref[...]
    recv_a[:, pl.ds(al(p * cap, 128), cap)] = lat_ref[pl.ds(al(c * half, 16), half), :]
    for o in range(1, n):
        s = lax.rem(p + o, n)
        arrived(split_all.at[pl.ds(al(s * 8, 8), 8), :], "split", s)

    info = split_all[...]
    rows8 = info.shape[0]
    item_a, count_a = info[:, 0:1], info[:, 1:2]
    item_b, count_b = info[:, 2:3], info[:, 3:4]
    lane = lax.broadcasted_iota(jnp.int32, (rows8, 128), 1).astype(f32)
    held = jnp.where(item_a == lane, count_a, 0.0) + jnp.where(item_b == lane, count_b, 0.0)
    row_i = lax.broadcasted_iota(jnp.int32, (rows8, rows8), 0)
    row_k = lax.broadcasted_iota(jnp.int32, (rows8, rows8), 1)
    lower = jnp.where((row_k % 8 == 0) & (row_k // 8 < row_i // 8), 1.0, 0.0)
    before = jnp.dot(lower.astype(bf16), held.astype(bf16), preferred_element_type=f32)
    base_a = jnp.sum(jnp.where(item_a == lane, before, 0.0), axis=1, keepdims=True)
    base_b = jnp.sum(jnp.where(item_b == lane, before, 0.0), axis=1, keepdims=True)
    base_b = base_b + jnp.where(item_b == item_a, count_a, 0.0)
    slot = lax.broadcasted_iota(jnp.int32, (rows8, cap), 1).astype(f32)
    t_ref[...] = jnp.where(
        slot < count_a,
        item_a * IMG + base_a + slot,
        jnp.where(slot < count_a + count_b, item_b * IMG + base_b + slot - count_a, -1.0),
    )
    want = (lax.broadcasted_iota(jnp.int32, (2 * comp, cap), 0) + pair * (2 * comp)).astype(f32)
    for s in range(n):
        m_ref[:, s * cap:(s + 1) * cap] = jnp.where(
            t_ref[s * 8:s * 8 + 1, :] == want, 1.0, 0.0
        ).astype(bf16)
    for k in range(2):
        mine = t_ref[pl.ds(al((2 * pair + k) * 8, 8), 8), :][0:1, :]
        for s in range(n):
            rows = (lax.broadcasted_iota(jnp.int32, (comp, cap), 0) + s * comp).astype(f32)
            e_ref[s * comp:(s + 1) * comp, k * cap:(k + 1) * cap] = jnp.where(
                mine == rows, 1.0, 0.0
            ).astype(bf16)
    gain_pad[...] = jnp.zeros_like(gain_pad)
    gain_pad[0:gains_ref.shape[0], 0:HEAD] = gains_ref[...]
    gain_ref = gain_pad[...].T[:HEAD, :]
    text_rows[...] = jnp.zeros_like(text_rows)
    for k in range(2):
        text_rows[0:txt, :] = texts_ref[item].astype(f32)[:, k, :]
        text_t[k] = text_rows[...].T.astype(bf16)

    def x_rows(z, core, part):
        return pl.ds(al(z * share + core * half + part[0], 16), part[1])

    for k, (start, size) in enumerate(parts):
        for o in range(1, n):
            s = lax.rem(p + o, n)
            arrived(recv_a.at[start:start + size, pl.ds(al(s * cap, 128), cap)], "a", 2 * s + k)
        chosen = lax.dot_general(
            recv_a[start:start + size, :], m_ref[...], (((1,), (1,)), ((), ())),
            preferred_element_type=f32,
        ).astype(bf16)
        sel[0, start:start + size, :] = chosen[:, :comp]
        sel[1, start:start + size, :] = chosen[:, comp:]
        mine = x_rows(m, c, (start, size))
        spot_b = 2 * (2 * m + c) + k
        for o in range(1, nz):
            z = lax.rem(m + o, nz)
            for q in range(2):
                push(sel.at[q, start:start + size, :], x_t.at[mine, :], "b", spot_b, (2 * pair + q, z))
        push(sel.at[1 - c, start:start + size, :], x_t.at[mine, :], "b", spot_b, (sib, m))
        x_t[mine, :] = sel[c, start:start + size, :]
    for k, part in enumerate(parts):
        arrived(x_t.at[x_rows(m, 1 - c, part), :], "b", 2 * (2 * m + 1 - c) + k)
        for o in range(1, nz):
            z = lax.rem(m + o, nz)
            for q in range(2):
                arrived(x_t.at[x_rows(z, q, part), :], "b", 2 * (2 * z + q) + k)
    x_all = x_t[...].astype(f32).T
    normed = (layer_norm(x_all) * (1.0 + mod(1)) + mod(0)).astype(bf16)
    loads[0].wait()
    for j, (gain_col, scale) in enumerate(((1, 1.0), (None, 1.0), (0, HEAD ** -0.5))):
        which = (1, 2, 0)[j]
        proj = jnp.dot(normed, wq[which], preferred_element_type=f32).T
        for h in range(cols // HEAD):
            rows = proj[h * HEAD:(h + 1) * HEAD]
            if gain_col is not None:
                rows = head_norm(rows, gain_ref[:, gain_col:gain_col + 1]) * scale
            if which == 0:
                q_t[h * HEAD:(h + 1) * HEAD, :] = rows.astype(bf16)
            else:
                kv_t[which - 1, h * HEAD:(h + 1) * HEAD, :] = rows.astype(bf16)
        if which > 0:
            for o in range(1, group):
                pos = lax.rem(gpos + o, group)
                push(
                    kv_t.at[which - 1, pl.ds(al(lax.rem(pos, 2) * hcols, 16), hcols), :],
                    kv_all.at[which - 1, :, pl.ds(al(gpos * comp, 128), comp)],
                    "kv", 2 * gpos + which - 1, (gbase + pos, m),
                )
            kv_all[which - 1, :, pl.ds(al(gpos * comp, 128), comp)] = kv_t[
                which - 1, pl.ds(al(c * hcols, 16), hcols), :
            ]
    push(
        q_t.at[pl.ds(al((1 - c) * hcols, 16), hcols), :],
        q_all.at[:, pl.ds(al(c * comp, 128), comp)], "q", 0, (sib, m),
    )
    q_all[:, pl.ds(al(c * comp, 128), comp)] = q_t[pl.ds(al(c * hcols, 16), hcols), :]

    text_pad = text_t.shape[2]
    text_k = text_t[0, pl.ds(al(c * hcols, 16), hcols), :].astype(f32)
    text_v = text_t[1, pl.ds(al(c * hcols, 16), hcols), :]
    arrived(q_all.at[:, pl.ds(al((1 - c) * comp, 128), comp)], "q", 0)
    live_text = lax.broadcasted_iota(jnp.int32, (text_pad, 2 * comp), 0) < txt
    numer, denom = [], []
    for h in range(heads_half):
        hs = slice(h * HEAD, (h + 1) * HEAD)
        keys = head_norm(text_k[hs], gain_ref[:, 2:3]).T.astype(bf16)
        scores = jnp.dot(keys, q_all[hs, :], preferred_element_type=f32)
        weights_t = jnp.where(live_text, jnp.exp(scores), 0.0)
        denom.append(jnp.sum(weights_t, axis=0, keepdims=True))
        numer.append(jnp.dot(text_v[hs], weights_t.astype(bf16), preferred_element_type=f32))
    def kv_arrived(k):
        for o in range(1, group):
            pos = lax.rem(gpos + o, group)
            arrived(kv_all.at[k, :, pl.ds(al(pos * comp, 128), comp)], "kv", 2 * pos + k)

    kv_arrived(0)
    low = []
    for h in range(heads_half):
        hs = slice(h * HEAD, (h + 1) * HEAD)
        keys = kv_all[0, hs, :].astype(f32).T.astype(bf16)
        weights_t = jnp.exp(jnp.dot(keys, q_all[hs, :], preferred_element_type=f32))
        denom[h] = denom[h] + jnp.sum(weights_t, axis=0, keepdims=True)
        low.append(weights_t.astype(bf16))
    kv_arrived(1)
    for h in range(heads_half):
        hs = slice(h * HEAD, (h + 1) * HEAD)
        mixed = numer[h] + jnp.dot(kv_all[1, hs, :], low[h], preferred_element_type=f32)
        attended = (mixed / denom[h]).astype(bf16)
        att_snd[0, hs, :] = attended[:, :comp]
        att_snd[1, hs, :] = attended[:, comp:]
    push(att_snd.at[1 - c], att_t.at[pl.ds(al(c * hcols, 16), hcols), :], "d", 0, (sib, m))
    att_t[pl.ds(al(c * hcols, 16), hcols), :] = att_snd[c]
    loads[1].wait()
    arrived(att_t.at[pl.ds(al((1 - c) * hcols, 16), hcols), :], "d", 0)

    halves = ((0, half), (half, share - half))
    line_sends = []

    def scatter_over_mlp(lhs, w_ref, gate_row, buf, recv, name, early):
        sent = 0
        for start, size in column_chunks(width, 256):
            block = jnp.dot(lhs, w_ref[:, start:start + size], preferred_element_type=f32)
            block = block * mods_ref[gate_row, item, :, start:start + size]
            buf[start:start + size, :] = block.T.astype(bf16)
            while early and sent < nz and (sent + 1) * share <= start + size:
                for k, part in enumerate(halves):
                    index = counter[0]
                    counter[0] += 1
                    copy = pltpu.make_async_remote_copy(
                        src_ref=buf.at[sent * share + part[0]:sent * share + part[0] + part[1], :],
                        dst_ref=recv.at[m, part[0]:part[0] + part[1], :],
                        send_sem=send_sem.at[index], recv_sem=recv_sem.at[rbase[name] + 2 * m + k],
                        device_id=(p, sent), device_id_type=MESH,
                    )

                    @pl.when(m != sent)
                    def _():
                        copy.start()
                    line_sends.append((m != sent, copy))
                sent += 1
        if not early:
            for k, part in enumerate(halves):
                for o in range(1, nz):
                    z = lax.rem(m + o, nz)
                    push(
                        buf.at[pl.ds(al(z * share + part[0], 16), part[1]), :],
                        recv.at[m, part[0]:part[0] + part[1], :], name, 2 * m + k, (p, z),
                    )

    def summed(buf, recv, name, k):
        start, size = halves[k]
        for o in range(1, nz):
            z = lax.rem(m + o, nz)
            arrived(recv.at[z, start:start + size, :], name, 2 * z + k)
        total = buf[pl.ds(al(m * share + start, 16), size), :].astype(f32)
        for o in range(1, nz):
            total = total + recv[lax.rem(m + o, nz), start:start + size, :].astype(f32)
        return total

    def line_hop(buf, name, s, k):
        start, size = halves[k]
        for way in (1, -1):
            block = m - way * s
            held_here = (block >= 0) & (block < nz)
            safe = lax.rem(block + nz, nz)
            index = counter[0]
            counter[0] += 1
            ref = buf.at[pl.ds(al(safe * share + start, 16), size), :]
            copy = pltpu.make_async_remote_copy(
                src_ref=ref, dst_ref=ref, send_sem=send_sem.at[index],
                recv_sem=recv_sem.at[rbase[name] + 2 * safe + k],
                device_id=(p, lax.rem(m + way + nz, nz)), device_id_type=MESH,
            )
            if s > 0:
                @pl.when(held_here)
                def _():
                    copy.wait_recv()
            if s < nz - 1:
                go = held_here & (m + way >= 0) & (m + way < nz)

                @pl.when(go)
                def _():
                    copy.start()
                line_sends.append((go, copy))

    attended = att_t[...].astype(f32).T.astype(bf16)
    scatter_over_mlp(attended, wo, 2, part_t, recv_e, "e", False)
    own_rows = [pl.ds(al(m * share + start, 16), size) for start, size in halves]
    for k in range(2):
        ga = summed(part_t, recv_e, "e", k)
        ga_own[halves[k][0]:halves[k][0] + halves[k][1], :] = ga
        ga_t[own_rows[k], :] = ga.astype(bf16)
        line_hop(ga_t, "f", 0, k)
    loads[2].wait()
    for s in range(1, nz):
        for k in range(2):
            line_hop(ga_t, "f", s, k)
    after = x_all + ga_t[...].astype(f32).T
    normed_two = (layer_norm(after) * (1.0 + mod(4)) + mod(3)).astype(bf16)
    hidden = []
    for start, size in column_chunks(wu.shape[1], 256):
        up = jnp.dot(normed_two, wu[:, start:start + size], preferred_element_type=f32)
        hidden.append(jax.nn.gelu(up, approximate=True).astype(bf16))
    hidden = jnp.concatenate(hidden, axis=1)
    loads[3].wait()
    scatter_over_mlp(hidden, wd, 5, mid_t, recv_g, "g", False)

    for k in range(2):
        gm = summed(mid_t, recv_g, "g", k)
        own = slice(halves[k][0], halves[k][0] + halves[k][1])
        x_own = x_t[own_rows[k], :].astype(f32)
        fin_t[own, :] = (x_own + step * (x_own + ga_own[own, :] + gm)).astype(bf16)
        for o in range(0, n, 2):
            d = lax.rem(pair * 2 + k + o, n)
            index = counter[0]
            counter[0] += 1
            copy = pltpu.make_async_remote_copy(
                src_ref=fin_t.at[own, :], dst_ref=recv_f.at[:, pl.ds(al(p * comp, 128), comp)],
                send_sem=send_sem.at[index], recv_sem=recv_sem.at[rbase["h"] + p],
                device_id=(d, m), device_id_type=MESH,
            )

            @pl.when(d != p)
            def _():
                copy.start()
            line_sends.append((d != p, copy))
    recv_f[:, pl.ds(al(p * comp, 128), comp)] = fin_t[pl.ds(al(c * half, 16), half), :]
    for o in range(1, n):
        s = lax.rem(p + o, n)
        arrived(recv_f.at[:, pl.ds(al(s * comp, 128), comp)], "h", s)
    spread = jnp.dot(recv_f[...], e_ref[...], preferred_element_type=f32).astype(bf16)
    res[0] = spread[:, :cap]
    res[1] = spread[:, cap:]
    push(res.at[1 - c], recv_i, "i", 0, (sib, m))
    out_ref[pl.ds(al(c * half, 16), half), :] = res[c]
    arrived(recv_i, "i", 0)
    out_ref[pl.ds(al((1 - c) * half, 16), half), :] = recv_i[...]
    for copy in sends:
        copy.wait_send()
    for go, copy in line_sends:
        @pl.when(go)
        def _():
            copy.wait_send()


def body(
    n, nz,
    latent, split_list, modulation, w_qkv, w_out, w_up, w_down, qk_gains, text_kv, timestep, step_sizes,
):
    cap, share = latent.shape
    width = share * nz
    items = modulation.shape[0]
    comp = items * IMG // n
    group = IMG // comp
    cols = w_out.shape[0]
    hcols = cols // 2
    hidden = w_up.shape[1]
    txt = text_kv.shape[2]
    text_pad = -(-txt // 128) * 128
    half = share // 2

    vmem = pl.BlockSpec(memory_space=pltpu.VMEM)
    smem = pl.BlockSpec(memory_space=pltpu.SMEM)
    hbm = pl.BlockSpec(memory_space=pl.ANY)
    recv_count = 4 * n + 10 * nz + 2 * group + 3
    send_count = 4 * n + 4 * nz + 2 * group + 16 * nz + n + 4
    out = pl.pallas_call(
        functools.partial(kernel, n, nz, txt),
        out_shape=jax.ShapeDtypeStruct((share, cap), bf16),
        in_specs=[vmem, smem, vmem, vmem, vmem, smem, smem] + [hbm] * 4,
        out_specs=vmem,
        scratch_shapes=[
            pltpu.VMEM((3, width, cols), bf16),
            pltpu.VMEM((cols, width), bf16),
            pltpu.VMEM((width, hidden), bf16),
            pltpu.VMEM((hidden, width), bf16),
            pltpu.VMEM((8, 128), f32),
            pltpu.VMEM((128, 128), f32),
            pltpu.VMEM((text_pad, cols), f32),
            pltpu.VMEM((2, cols, text_pad), bf16),
            pltpu.VMEM((n * 8, 128), f32),
            pltpu.VMEM((n * 8, cap), f32),
            pltpu.VMEM((half, n * cap), bf16),
            pltpu.VMEM((2 * comp, n * cap), bf16),
            pltpu.VMEM((n * comp, 2 * cap), bf16),
            pltpu.VMEM((2, half, comp), bf16),
            pltpu.VMEM((width, comp), bf16),
            pltpu.VMEM((cols, comp), bf16),
            pltpu.VMEM((2, cols, comp), bf16),
            pltpu.VMEM((hcols, 2 * comp), bf16),
            pltpu.VMEM((2, hcols, group * comp), bf16),
            pltpu.VMEM((2, hcols, comp), bf16),
            pltpu.VMEM((cols, comp), bf16),
            pltpu.VMEM((width, comp), bf16),
            pltpu.VMEM((nz, share, comp), bf16),
            pltpu.VMEM((width, comp), bf16),
            pltpu.VMEM((share, comp), f32),
            pltpu.VMEM((width, comp), bf16),
            pltpu.VMEM((nz, share, comp), bf16),
            pltpu.VMEM((share, comp), bf16),
            pltpu.VMEM((half, n * comp), bf16),
            pltpu.VMEM((2, half, cap), bf16),
            pltpu.VMEM((half, cap), bf16),
            pltpu.SemaphoreType.DMA((4,)),
            pltpu.SemaphoreType.DMA((send_count,)),
            pltpu.SemaphoreType.DMA((recv_count,)),
        ],
        compiler_params=pltpu.CompilerParams(
            collective_id=0, has_side_effects=True, vmem_limit_bytes=58 * 1024 * 1024
        ),
    )(latent.T, split_list, jnp.swapaxes(modulation, 0, 1)[:, :, None, :], qk_gains, jnp.transpose(text_kv, (1, 2, 0, 3)), timestep, step_sizes, jnp.swapaxes(w_qkv, 0, 1), w_out, w_up, w_down)
    return out.T


def solution(mesh):
    return jax.shard_map(
        functools.partial(body, mesh.shape["patch"], mesh.shape["mlp"]),
        mesh=mesh,
        in_specs=(
            P("patch", "mlp"),
            P("patch", None),
            P(),
            P(None, None, "mlp"),
            P("mlp", None),
            P(None, "mlp"),
            P("mlp", None),
            P(),
            P(None, None, None, "mlp"),
            P(),
            P(),
        ),
        out_specs=P("patch", "mlp"),
        check_vma=False,
    )
```
